512 devices in a mesh: dp: 32 (over y, x, core), sp: 16 (over z).
Axes of the slice: x: 4, y: 4, z: 16, core: 2. Of those that a mesh axis runs over, the one named last changes fastest.
Arguments:
- queries: bfloat16 [32768, 4096], P(('dp', 'sp'))
- keys: bfloat16 [32768, 1024], P(('dp', 'sp'))
- values: bfloat16 [32768, 1024], P(('dp', 'sp')), may hold values from -6 to 6
- positions: int32 [32768], P(('dp', 'sp')), may hold values from 0 to 1023, as said below
- piece_lengths: int32 [32, 16, 1], P('dp', 'sp'), may hold values from 1 to 64, as said below
- dest_group: int32 [32, 1], P('dp'), may hold values from 0 to 31, as said below
- dest_offset: int32 [32, 16, 1], P('dp', 'sp'), may hold values from 0 to 0, as said below
Outputs:
- packed_out: bfloat16 [32768, 4096], P(('dp', 'sp'))
The draws below stay inside these ranges and needn't reach their ends.
Inputs may be any that keep to these rules, and one draw needn't show every extreme that they name: `piece_lengths`: the pieces of one sequence over the 16 devices of its instance sum to its length, which is 512 or more; the rows of a piece are the slot's first rows. dest_group[i, s] is i XOR m_s, where the numbers m_s depend on the slot s alone and differ from slot to slot; so every packed group is named by exactly one entry. `dest_offset`: on one device, the pieces arriving at one group lie back to back from row 0 in order of source instance and end at or before 64; in every draw some group is filled to exactly 64 rows on every device. The live rows of one sequence, over all its devices, hold the positions 0 to its length - 1, each once; rows that are not live hold 0.
All inputs are finite; a program needn't handle non-finite values.
Results may differ from the reference program's by a relative error of at most 0.0061.
Values may be sent and summed in bfloat16 or wider, within the bound.
A program may use at most 64 MiB of HBM per device.

```python
import jax
import jax.numpy as jnp
from jax import lax

QUERY_HEADS = 32
KEY_VALUE_HEADS = 8
HEAD_SIZE = 128
DEVICE_ROW_LIMIT = 64
GROUP_SEQUENCES = 1
DECODE_GROUPS = 32
SHARDS = 16
SLOTS = 64
GROUP_ROWS = 1024
TOTAL_ROWS = 32768


def plan_layout(key):
    inner = jax.random.fold_in(key, 5)
    key_shift, key_full, key_total, key_rot = jax.random.split(inner, 4)
    masks = jax.random.permutation(key_shift, DECODE_GROUPS)[:GROUP_SEQUENCES].astype(jnp.int32)
    destination = jnp.bitwise_xor(jnp.arange(DECODE_GROUPS, dtype=jnp.int32)[:, None], masks[None, :]).astype(jnp.int32)
    full_group = jax.random.randint(key_full, (), 0, DECODE_GROUPS)
    seq_total = jax.random.randint(key_total, (DECODE_GROUPS, GROUP_SEQUENCES), SHARDS * DEVICE_ROW_LIMIT // 2, SHARDS * DEVICE_ROW_LIMIT + 1)
    seq_total = jnp.where(destination == full_group, SHARDS * DEVICE_ROW_LIMIT, seq_total).astype(jnp.int32)
    rotation = jax.random.randint(key_rot, (DECODE_GROUPS, GROUP_SEQUENCES), 0, SHARDS)
    column = jnp.arange(SHARDS, dtype=jnp.int32)[None, :, None]
    first_token = (column - rotation[:, None, :]) % SHARDS
    lengths = ((seq_total[:, None, :] - first_token + SHARDS - 1) // SHARDS).astype(jnp.int32)
    onehot = (destination[:, :, None] == jnp.arange(DECODE_GROUPS, dtype=jnp.int32)[None, None, :]).astype(jnp.int32)
    arrive = jnp.sum(lengths[:, :, :, None] * onehot[:, None, :, :], axis=2)
    starts = jnp.cumsum(arrive, axis=0) - arrive
    offsets = jnp.take_along_axis(starts, jnp.broadcast_to(destination[:, None, :], lengths.shape), axis=2).astype(jnp.int32)
    row_index = jnp.arange(DEVICE_ROW_LIMIT, dtype=jnp.int32)
    spots = jnp.where(row_index[None, None, None, :] < lengths[..., None], row_index[None, None, None, :] * SHARDS + first_token[..., None], 0)
    return (destination, lengths, offsets, spots.reshape(TOTAL_ROWS).astype(jnp.int32))


def draw_queries(key, part):
    local_key_rows = jax.random.fold_in(key, 31)
    attention_output = jax.random.normal(local_key_rows, (TOTAL_ROWS, QUERY_HEADS, HEAD_SIZE), jnp.float32)
    return attention_output.reshape(TOTAL_ROWS, QUERY_HEADS * HEAD_SIZE).astype(jnp.bfloat16)


def draw_keys(key, part):
    local_key_rows = jax.random.fold_in(key, 21)
    attention_output = jax.random.normal(local_key_rows, (TOTAL_ROWS, KEY_VALUE_HEADS, HEAD_SIZE), jnp.float32)
    return attention_output.reshape(TOTAL_ROWS, KEY_VALUE_HEADS * HEAD_SIZE).astype(jnp.bfloat16)


def draw_positions(key, part):
    return plan_layout(key)[3]


def draw_piece_lengths(key, part):
    return plan_layout(key)[1]


def draw_dest_group(key, part):
    return plan_layout(key)[0]


def draw_dest_offset(key, part):
    return plan_layout(key)[2]


def steps_of(rng, shape, cuts, low, largest):
    loudness = 1.0
    for dim, parts in cuts:
        draws = jax.random.uniform(jax.random.fold_in(jax.random.fold_in(rng, 6), dim), (parts,), jnp.float32, low / len(cuts), largest / len(cuts))
        loudness = loudness * jnp.repeat(jnp.exp(draws), shape[dim] // parts).reshape((-1,) + (1,) * (len(shape) - 1 - dim))
    return loudness


def scatter_about(key, extent, scale, bound, shards=(), kind=jnp.bfloat16):
    drawn = scale * jax.random.normal(key, extent, jnp.float32)
    if shards:
        drawn = drawn * steps_of(key, extent, shards, -0.22, 0.18)
    return jnp.clip(drawn, -bound, bound).astype(kind)


def setup_inputs(seed: int = 0) -> dict:
    seeds = jax.random.split(jax.random.key(seed), 8)
    return {
        "queries": draw_queries(jax.random.fold_in(seeds[7], 71), 0),
        "keys": draw_keys(jax.random.fold_in(seeds[7], 71), 0),
        "values": scatter_about(seeds[2], (TOTAL_ROWS, KEY_VALUE_HEADS * HEAD_SIZE), 1.0, 6.0, ((0, 512),)),
        "positions": draw_positions(jax.random.fold_in(seeds[7], 71), 0),
        "piece_lengths": draw_piece_lengths(jax.random.fold_in(seeds[7], 71), 0),
        "dest_group": draw_dest_group(jax.random.fold_in(seeds[7], 71), 0),
        "dest_offset": draw_dest_offset(jax.random.fold_in(seeds[7], 71), 0),
    }


THETA = 1000000.0
NEG = -1.0e30


def apply_rotary(heads_in, row_pos):
    half_width = heads_in.shape[-1] // 2
    frequency = THETA ** (-(jnp.arange(half_width, dtype=jnp.float32) * 2.0 / heads_in.shape[-1]))
    angles = row_pos.astype(jnp.float32)[:, None] * frequency[None, :]
    cosine = jnp.cos(angles)[:, None, :]
    sines = jnp.sin(angles)[:, None, :]
    widened = heads_in.astype(jnp.float32)
    first_half = widened[..., :half_width]
    second_half = widened[..., half_width:]
    return jnp.concatenate([first_half * cosine - second_half * sines, second_half * cosine + first_half * sines], axis=-1).astype(jnp.bfloat16)


def masked_block(query_rows, query_pos, query_seg, key_collection, value_collection, key_pos, key_seg):
    scale = query_rows.shape[-1] ** -0.5
    scores = jnp.einsum('qhd,khd->hqk', query_rows, key_collection, preferred_element_type=jnp.float32) * scale
    allowed = (query_seg[:, None] == key_seg[None, :]) & (query_seg[:, None] >= 0) & (key_pos[None, :] <= query_pos[:, None])
    row_max = jnp.max(jnp.where(allowed[None], scores, NEG), axis=-1, keepdims=True)
    weight = jnp.where(allowed[None], jnp.exp(scores - row_max), 0.0)
    weight_sum = jnp.sum(weight, axis=-1)
    attended = jnp.einsum('hqk,khd->qhd', weight.astype(jnp.bfloat16), value_collection, preferred_element_type=jnp.float32)
    live_rows = query_seg >= 0
    divisor = jnp.where(live_rows[None, :], weight_sum, 1.0)
    attention_output = attended / jnp.transpose(divisor)[:, :, None]
    return jnp.where(live_rows[:, None, None], attention_output, 0.0).astype(jnp.bfloat16)


def attend_blocks(rot_q, rotated_keys, rotated_values, group_positions, group_seg):
    span_rows = rot_q.shape[0]
    block_rows = min(512, span_rows)
    block_count = span_rows // block_rows

    def one_block(block_args):
        query_rows, query_pos, query_seg = block_args
        return masked_block(query_rows, query_pos, query_seg, rotated_keys, rotated_values, group_positions, group_seg)

    outputs = lax.map(one_block, (rot_q.reshape(block_count, block_rows, rot_q.shape[1], rot_q.shape[2]), group_positions.reshape(block_count, block_rows), group_seg.reshape(block_count, block_rows)))
    return outputs.reshape(rot_q.shape)


def reference(queries, keys, values, positions, piece_lengths, dest_group, dest_offset):
    row_index = jnp.arange(DEVICE_ROW_LIMIT, dtype=jnp.int32)
    live_rows = row_index[None, None, None, :] < piece_lengths[:, :, :, None]
    column = jnp.arange(SHARDS, dtype=jnp.int32)[None, :, None, None]
    group_index = dest_group[:, None, :, None]
    packed_index = (group_index * SHARDS + column) * SLOTS + dest_offset[:, :, :, None] + row_index[None, None, None, :]
    packed_index = jnp.where(live_rows, packed_index, TOTAL_ROWS).reshape(TOTAL_ROWS).astype(jnp.int32)
    instance = jnp.broadcast_to(jnp.arange(DECODE_GROUPS, dtype=jnp.int32)[:, None, None, None], (DECODE_GROUPS, SHARDS, GROUP_SEQUENCES, DEVICE_ROW_LIMIT)).reshape(TOTAL_ROWS)

    def distribute_rows(array, fill_value):
        filled = jnp.full((TOTAL_ROWS + 1,) + array.shape[1:], fill_value, array.dtype)
        return filled.at[packed_index].set(array)[:TOTAL_ROWS]

    packed_q = distribute_rows(queries, 0).reshape(DECODE_GROUPS, GROUP_ROWS, QUERY_HEADS, HEAD_SIZE)
    packed_keys = distribute_rows(keys, 0).reshape(DECODE_GROUPS, GROUP_ROWS, KEY_VALUE_HEADS, HEAD_SIZE)
    packed_values = distribute_rows(values, 0).reshape(DECODE_GROUPS, GROUP_ROWS, KEY_VALUE_HEADS, HEAD_SIZE)
    packed_pos = distribute_rows(positions, 0).reshape(DECODE_GROUPS, GROUP_ROWS)
    packed_seg = distribute_rows(instance, -1).reshape(DECODE_GROUPS, GROUP_ROWS)

    def per_group(group_args):
        group_q, group_keys, group_values, group_positions, group_seg = group_args
        rot_q = apply_rotary(group_q, group_positions)
        rotated_keys = jnp.repeat(apply_rotary(group_keys, group_positions), QUERY_HEADS // KEY_VALUE_HEADS, axis=1)
        rotated_values = jnp.repeat(group_values, QUERY_HEADS // KEY_VALUE_HEADS, axis=1)
        return attend_blocks(rot_q, rotated_keys, rotated_values, group_positions, group_seg)

    outputs = lax.map(per_group, (packed_q, packed_keys, packed_values, packed_pos, packed_seg))
    return outputs.reshape(TOTAL_ROWS, QUERY_HEADS * HEAD_SIZE)
```

```python
import functools

import jax
import jax.numpy as jnp
import numpy as np
from jax import lax
from jax.experimental import pallas as pl
from jax.experimental.pallas import tpu as pltpu
from jax.sharding import PartitionSpec as P

QH = 32
KVH = 8
D = 128
ROWS = 64
REP = QH // KVH
THETA = 1000000.0
NEG = -1.0e30
FAR = 1 << 30
MESH = pl.DeviceIdType.MESH


def frequencies():
    half = THETA ** (-(np.arange(D // 2, dtype=np.float64) * 2.0 / D))
    return np.concatenate([half, half])[None, :].astype(np.float32)


def kernel(n, len_ref, q_ref, k_ref, v_ref, pos_ref, freq_ref, out_ref,
           kv, kp, rq, cap, send_r, send_l, recv, psend_r, psend_l, precv):
    z = lax.axis_index("sp")
    dp = lax.axis_index("dp")
    right, left = lax.rem(z + 1, n), lax.rem(z + n - 1, n)
    half = n // 2
    HB = KVH // 2
    barrier = pltpu.get_barrier_semaphore()
    for peer in (left, right):
        pl.semaphore_signal(barrier, inc=1, device_id=(dp, peer), device_id_type=MESH)

    length = len_ref[0]
    rows = lax.broadcasted_iota(jnp.int32, (ROWS, D), 0)
    lanes = lax.broadcasted_iota(jnp.int32, (ROWS, D), 1)
    diag = rows == lax.rem(lanes, ROWS)
    live = rows < length
    pos_wide = jnp.concatenate([pos_ref[...], pos_ref[...]], axis=1)
    pos_col = jnp.sum(
        jnp.where((rows == lanes), jnp.broadcast_to(pos_wide, (ROWS, D)), 0), axis=1, keepdims=True
    )
    angle = pos_col.astype(jnp.float32) * freq_ref[...]
    cosine = jnp.cos(angle)
    sine = jnp.sin(angle)
    sine = jnp.where(lanes < D // 2, -sine, sine)

    def rotate(x):
        x = x.astype(jnp.float32)
        return x * cosine + pltpu.roll(x, D // 2, 1) * sine

    for h in range(KVH):
        cols = pl.ds(h * D, D)
        rk = jnp.where(live, rotate(k_ref[:, cols]), 0.0)
        kv[h, z, 0] = rk.astype(jnp.bfloat16)
        kv[h, z, 1] = v_ref[:, cols]
    key_pos = jnp.where(diag & live & (lanes // ROWS == lax.rem(z, 2)), pos_col, FAR)
    kp[z] = jnp.broadcast_to(jnp.min(key_pos, axis=0, keepdims=True), (8, D))

    pl.semaphore_wait(barrier, 2)

    def reach(h):
        return (half, n - 1 - half) if h % 2 == 0 else (n - 1 - half, half)

    def copy(h, d, to_right):
        shard = lax.rem(z - d + n, n) if to_right else lax.rem(z + d, n)
        peer = right if to_right else left
        return pltpu.make_async_remote_copy(
            src_ref=kv.at[h, shard], dst_ref=kv.at[h, shard],
            send_sem=(send_r if to_right else send_l).at[h, d],
            recv_sem=recv.at[h, shard],
            device_id=(dp, peer), device_id_type=MESH,
        )

    def pcopy(d, to_right):
        shard = lax.rem(z - d + n, n) if to_right else lax.rem(z + d, n)
        peer = right if to_right else left
        return pltpu.make_async_remote_copy(
            src_ref=kp.at[shard], dst_ref=kp.at[shard],
            send_sem=(psend_r if to_right else psend_l).at[d],
            recv_sem=precv.at[shard],
            device_id=(dp, peer), device_id_type=MESH,
        )

    def step(block, d, with_pos):
        for dir_right in (True, False):
            if with_pos:
                r = reach(0)[0 if dir_right else 1]

                @pl.when((d >= 1) & (d <= r))
                def _():
                    pcopy(d, dir_right).wait_recv()

                @pl.when(d < r)
                def _():
                    pcopy(d, dir_right).start()
        for hh in range(HB):
            h = block * HB + hh
            for dir_right in (True, False):
                r = reach(hh)[0 if dir_right else 1]

                @pl.when((d >= 1) & (d <= r))
                def _():
                    copy(h, d, dir_right).wait_recv()

                @pl.when(d < r)
                def _():
                    copy(h, d, dir_right).start()

    def rotate_q(h):
        for g in range(REP):
            cols = pl.ds((h * REP + g) * D, D)
            rq[h, g * ROWS:(g + 1) * ROWS] = rotate(q_ref[:, cols]).astype(jnp.bfloat16)

    scale = float(D ** -0.5 * np.log2(np.e))

    def attention(h, part):
        keys = kv[h, :, 0].reshape(n * ROWS, D)
        vals = kv[h, :, 1].reshape(n * ROWS, D)
        rows_p = pl.ds(part * 2 * ROWS, 2 * ROWS)
        s = lax.dot_general(rq[h, rows_p], keys, (((1,), (1,)), ((), ())),
                            preferred_element_type=jnp.float32)
        c = cap[...]
        s = jnp.minimum(s, jnp.concatenate([c, c], axis=0))
        m = jnp.max(s, axis=1, keepdims=True)
        w = jnp.exp2(s * scale - m * scale)
        total = jnp.sum(w, axis=1, keepdims=True)
        o = jnp.dot(w.astype(jnp.bfloat16), vals, preferred_element_type=jnp.float32)
        o = o / total
        for g in range(2):
            piece = jnp.where(live, o[g * ROWS:(g + 1) * ROWS], 0.0).astype(jnp.bfloat16)
            out_ref[h * REP + part * 2 + g] = piece

    def first(d, _):
        step(0, d, True)

        @pl.when(d == 0)
        def _():
            for h in range(KVH):
                rotate_q(h)
        return 0

    lax.fori_loop(0, half + 1, first, 0)
    step(1, 0, False)
    for t in range(n // 2):
        pair = jnp.minimum(kp[2 * t, 0:1], kp[2 * t + 1, 0:1])
        cap[:, t * D:(t + 1) * D] = jnp.where(
            jnp.broadcast_to(pair, (ROWS, D)) <= pos_col, jnp.float32(jnp.inf), NEG)

    def second(d, _):
        step(1, d, False)
        u = d - 1
        attention(lax.div(u, 2), lax.rem(u, 2))
        return 0

    lax.fori_loop(1, half + 1, second, 0)

    def last(u, _):
        attention(HB + lax.div(u, 2), lax.rem(u, 2))
        return 0

    lax.fori_loop(0, 2 * HB, last, 0)

    def drain(d, _):
        for h in range(KVH):
            for dir_right in (True, False):
                @pl.when(d < reach(h)[0 if dir_right else 1])
                def _():
                    copy(h, d, dir_right).wait_send()
        for dir_right in (True, False):
            @pl.when(d < reach(0)[0 if dir_right else 1])
            def _():
                pcopy(d, dir_right).wait_send()
        return 0

    lax.fori_loop(0, half, drain, 0)


def on_device(queries, keys, values, positions, piece_lengths, dest_group, dest_offset):
    n = lax.axis_size("sp")
    groups = lax.axis_size("dp")
    vm = pl.BlockSpec(memory_space=pltpu.VMEM)
    sm = pl.BlockSpec(memory_space=pltpu.SMEM)
    dma = pltpu.SemaphoreType.DMA
    out = pl.pallas_call(
        functools.partial(kernel, n),
        out_shape=jax.ShapeDtypeStruct((QH, ROWS, D), jnp.bfloat16),
        in_specs=[sm, vm, vm, vm, vm, vm],
        out_specs=vm,
        scratch_shapes=[
            pltpu.VMEM((KVH, n, 2, ROWS, D), jnp.bfloat16),
            pltpu.VMEM((n, 8, D), jnp.int32),
            pltpu.VMEM((KVH, REP * ROWS, D), jnp.bfloat16),
            pltpu.VMEM((ROWS, n * ROWS), jnp.float32),
            dma((KVH, n)), dma((KVH, n)), dma((KVH, n)),
            dma((n,)), dma((n,)), dma((n,)),
        ],
        compiler_params=pltpu.CompilerParams(
            collective_id=0, has_side_effects=True, vmem_limit_bytes=40 * 1024 * 1024),
        name="gather_attend",
    )(piece_lengths.reshape(1), queries, keys, values, positions.reshape(1, ROWS),
      jnp.asarray(frequencies()))
    out = out.transpose(1, 0, 2).reshape(ROWS, QH * D)
    mask = dest_group[0, 0] ^ lax.axis_index("dp")
    return lax.switch(mask, [
        functools.partial(lambda m, x: lax.ppermute(x, "dp", [(i, i ^ m) for i in range(groups)]), m)
        for m in range(groups)
    ], out)


def solution(mesh):
    in_specs = (
        P(("dp", "sp"), None), P(("dp", "sp"), None), P(("dp", "sp"), None), P(("dp", "sp")),
        P("dp", "sp", None), P("dp", None), P("dp", "sp", None),
    )
    return jax.shard_map(on_device, mesh=mesh, in_specs=in_specs,
                         out_specs=P(("dp", "sp"), None), check_vma=False)
```

```python
import functools

import jax
import jax.numpy as jnp
import numpy as np
from jax import lax
from jax.experimental import pallas as pl
from jax.experimental.pallas import tpu as pltpu
from jax.sharding import PartitionSpec as P

QH = 32
KVH = 8
D = 128
ROWS = 64
REP = QH // KVH
QROWS = REP * ROWS
THETA = 1000000.0
NEG = -1.0e30
FAR = 1 << 30
DIRECT = 4
SCALE = float(D ** -0.5 * np.log2(np.e))
MESH = pl.DeviceIdType.MESH


def frequencies():
    half = THETA ** (-(np.arange(D // 2, dtype=np.float64) * 2.0 / D))
    return np.concatenate([half, half])[None, :].astype(np.float32)


def kernel(n, mask, len_ref, q_ref, k_ref, v_ref, pos_ref, freq_ref, out_ref,
           kraw, vraw, qraw, praw, fraw, src, kpsrc, qsrc, kv, kp, rq, cap, o1, m1, l1,
           load, ksend, krecv, own_send, own_recv, psend, precv, pown_send, pown_recv, qsend, qrecv):
    z = lax.axis_index("sp")
    dp = lax.axis_index("dp")
    far = dp
    for bit in range(5):
        if mask >> bit & 1:
            far = far + (1 << bit) * (1 - 2 * lax.rem(lax.div(dp, 1 << bit), 2))
    right, left = lax.rem(z + 1, n), lax.rem(z + n - 1, n)
    half = n // 2
    OWN = half - 2
    FIRST = 3 * n // 4

    loads = [
        pltpu.make_async_copy(pos_ref, praw, load.at[0]),
        pltpu.make_async_copy(freq_ref, fraw, load.at[1]),
        pltpu.make_async_copy(k_ref, kraw, load.at[2]),
        pltpu.make_async_copy(v_ref, vraw, load.at[3]),
        pltpu.make_async_copy(q_ref, qraw, load.at[4]),
    ]
    for c in loads:
        c.start()
    peers = [(dp, left), (dp, right)]
    if mask:
        peers += [(far, z), (far, left), (far, right)]
    barrier = pltpu.get_barrier_semaphore()
    for peer in peers:
        pl.semaphore_signal(barrier, inc=1, device_id=peer, device_id_type=MESH)

    length = len_ref[0]
    rows = lax.broadcasted_iota(jnp.int32, (ROWS, D), 0)
    lanes = lax.broadcasted_iota(jnp.int32, (ROWS, D), 1)
    diag = rows == lax.rem(lanes, ROWS)
    live = rows < length
    loads[0].wait()
    loads[1].wait()
    pos_wide = jnp.broadcast_to(jnp.concatenate([praw[...], praw[...]], axis=1), (ROWS, D))
    pos_col = jnp.sum(jnp.where(rows == lanes, pos_wide, 0), axis=1, keepdims=True)
    angle = pos_col.astype(jnp.float32) * fraw[...]
    cosine = jnp.cos(angle)
    sine = jnp.sin(angle)
    sine = jnp.where(lanes < D // 2, -sine, sine)

    def rotate(x):
        x = x.astype(jnp.float32)
        return x * cosine + pltpu.roll(x, D // 2, 1) * sine

    key_pos = jnp.min(jnp.where(diag & live, pos_col, FAR), axis=0, keepdims=True)
    key_pos = jnp.broadcast_to(key_pos, (8, D))
    if mask:
        kpsrc[...] = key_pos
    else:
        kp[OWN] = key_pos
    loads[2].wait()
    loads[3].wait()
    for h in range(KVH):
        cols = pl.ds(h * D, D)
        rk = jnp.where(live, rotate(kraw[:, cols]), 0.0).astype(jnp.bfloat16)
        if mask:
            src[h, 0] = rk
            src[h, 1] = vraw[:, cols]
        else:
            kv[h, OWN, 0] = rk
            kv[h, OWN, 1] = vraw[:, cols]

    def slot(s):
        return lax.rem(s + OWN, n)

    def reach(h):
        return (half, n - 1 - half) if h % 2 == 0 else (n - 1 - half, half)

    def remote(a, b, s, r, device):
        return pltpu.make_async_remote_copy(
            src_ref=a, dst_ref=b, send_sem=s, recv_sem=r, device_id=device, device_id_type=MESH)

    def at(d, to_right):
        return slot(d) if to_right else slot(n - d)

    def copy(h, d, to_right):
        a, b = at(d, to_right), at(d + 1, to_right)
        return remote(kv.at[h, a], kv.at[h, b], ksend.at[0 if to_right else 1, h, d],
                      krecv.at[h, b], (dp, right if to_right else left))

    def pcopy(d, to_right):
        a, b = at(d, to_right), at(d + 1, to_right)
        return remote(kp.at[a], kp.at[b], psend.at[0 if to_right else 1, d],
                      precv.at[b], (dp, right if to_right else left))

    def own(h):
        return remote(src.at[h], kv.at[h, OWN], own_send.at[h, 0], own_recv.at[h], (far, z))

    def direct(h, to_right):
        b = at(1, to_right)
        return remote(src.at[h], kv.at[h, b], own_send.at[h, 1 if to_right else 2],
                      krecv.at[h, b], (far, right if to_right else left))

    def pown():
        return remote(kpsrc, kp.at[OWN], pown_send.at[0], pown_recv.at[0], (far, z))

    def pdirect(to_right):
        b = at(1, to_right)
        return remote(kpsrc, kp.at[b], pown_send.at[1 if to_right else 2],
                      precv.at[b], (far, right if to_right else left))

    def qcopy(h):
        return remote(qsrc.at[h], rq.at[h], qsend.at[h], qrecv.at[h], (far, z))

    pl.semaphore_wait(barrier, len(peers))

    BOTH = (True, False)
    straight = DIRECT if mask else 0
    if mask:
        for h in range(straight):
            direct(h, True).start()
            direct(h, False).start()
            if h == 0:
                for h2 in range(straight, KVH):
                    own(h2).start()
        for r in BOTH:
            pdirect(r).start()
        pown().start()
        for h in range(straight):
            own(h).start()
    else:
        for r in BOTH:
            pcopy(0, r).start()
    for h in range(straight, KVH):
        if mask:
            own(h).wait_recv()
        for r in BOTH:
            copy(h, 0, r).start()

    def step(d):
        for r in BOTH:
            pcopy(d - 1, r).wait_recv()
            pcopy(d, r).start()
        for h in range(KVH):
            for r in BOTH:
                copy(h, d - 1, r).wait_recv()
                copy(h, d, r).start()

    loads[4].wait()

    def early(d, _):
        step(d)
        for e in range(2):
            h = (d - 1) * 2 + e
            for g in range(REP):
                cols = pl.ds(pl.multiple_of((h * REP + g) * D, D), D)
                x = rotate(qraw[:, cols]).astype(jnp.bfloat16)
                if mask:
                    qsrc[h, g * ROWS:(g + 1) * ROWS] = x
                else:
                    rq[h, g * ROWS:(g + 1) * ROWS] = x
            if mask:
                qcopy(h).start()
        return 0

    lax.fori_loop(1, 5, early, 0)

    def middle(d, _):
        step(d)
        return 0

    lax.fori_loop(5, half - 2, middle, 0)

    if mask:
        pown().wait_recv()
        for h in range(straight):
            own(h).wait_recv()
    q_row = kp[OWN][0:1]
    q_col = jnp.min(jnp.where(rows == lanes, jnp.broadcast_to(q_row, (ROWS, D)), FAR),
                    axis=1, keepdims=True)
    q_live = q_col < FAR

    def build_cap(first, last):
        for t in range(first // 2, last // 2):
            pair = jnp.where(lanes[0:1] < ROWS, kp[2 * t, 0:1], kp[2 * t + 1, 0:1])
            cap[:, t * D:(t + 1) * D] = jnp.where(
                jnp.broadcast_to(pair, (ROWS, D)) <= q_col, jnp.float32(jnp.inf), NEG)

    def scores(h, first, last):
        keys = kv[h, first:last, 0].reshape((last - first) * ROWS, D)
        s = lax.dot_general(rq[h], keys, (((1,), (1,)), ((), ())),
                            preferred_element_type=jnp.float32)
        c = cap[:, first * ROWS:last * ROWS]
        s = jnp.minimum(s, jnp.concatenate([c] * REP, axis=0))
        return s, jnp.max(s, axis=1, keepdims=True)

    def weigh(h, s, m, first, last):
        vals = kv[h, first:last, 1].reshape((last - first) * ROWS, D)
        w = jnp.exp2(s * SCALE - m * SCALE)
        return jnp.sum(w, axis=1, keepdims=True), jnp.dot(
            w.astype(jnp.bfloat16), vals, preferred_element_type=jnp.float32)

    def part_one(h):
        if mask:
            qcopy(h).wait_recv()
        s, m = scores(h, 0, FIRST)
        total, o = weigh(h, s, m, 0, FIRST)
        o1[h] = o
        m1[h] = jnp.broadcast_to(m, (QROWS, D))
        l1[h] = jnp.broadcast_to(total, (QROWS, D))

    def part_two(h):
        s, m = scores(h, FIRST, n)
        m = jnp.maximum(m, m1[h][:, 0:1])
        total, o = weigh(h, s, m, FIRST, n)
        a = jnp.exp2((m1[h] - m) * SCALE)
        o = (o1[h] * a + o) / (l1[h] * a + total)
        parts = [jnp.where(q_live, o[g * ROWS:(g + 1) * ROWS], 0.0) for g in range(REP)]
        out_ref[:, pl.ds(pl.multiple_of(h * REP * D, D), REP * D)] = jnp.concatenate(
            parts, axis=1).astype(jnp.bfloat16)

    d = half - 2
    for r in BOTH:
        pcopy(d - 1, r).wait_recv()
        pcopy(d, r).start()
    build_cap(0, FIRST)

    def six(j, _):
        for e in range(2):
            h = 2 * j + e
            for r in BOTH:
                copy(h, d - 1, r).wait_recv()
                copy(h, d, r).start()
        part_one(j)
        return 0

    lax.fori_loop(0, KVH // 2, six, 0)
    for r in BOTH:
        pcopy(d, r).wait_recv()
    pcopy(d + 1, True).start()

    def seven(j, _):
        for e in range(2):
            h = 2 * j + e
            for r in BOTH:
                copy(h, d, r).wait_recv()
            copy(h, d + 1, e == 0).start()
        part_one(KVH // 2 + j)
        return 0

    lax.fori_loop(0, KVH // 2, seven, 0)
    pcopy(d + 1, True).wait_recv()
    build_cap(FIRST, n)

    def eight(j, _):
        for e in range(2):
            h = 2 * j + e
            copy(h, d + 1, e == 0).wait_recv()
            part_two(h)
        return 0

    lax.fori_loop(0, KVH // 2, eight, 0)

    if mask:
        for r in BOTH:
            pdirect(r).wait_send()
        pown().wait_send()
        for h in range(KVH):
            own(h).wait_send()
            qcopy(h).wait_send()
        for h in range(straight):
            for r in BOTH:
                direct(h, r).wait_send()
    else:
        for r in BOTH:
            pcopy(0, r).wait_send()
    for h in range(straight, KVH):
        for r in BOTH:
            copy(h, 0, r).wait_send()

    def drain(d, _):
        for r in BOTH:
            pcopy(d, r).wait_send()
            for h in range(KVH):
                copy(h, d, r).wait_send()
        return 0

    lax.fori_loop(1, half - 1, drain, 0)
    pcopy(half - 1, True).wait_send()
    for h in range(KVH):
        copy(h, half - 1, h % 2 == 0).wait_send()


def attend(mask, n, *operands):
    vm = pl.BlockSpec(memory_space=pltpu.VMEM)
    sm = pl.BlockSpec(memory_space=pltpu.SMEM)
    hbm = pl.BlockSpec(memory_space=pl.ANY)
    dma = pltpu.SemaphoreType.DMA
    b16, f32, i32 = jnp.bfloat16, jnp.float32, jnp.int32
    half = n // 2
    return pl.pallas_call(
        functools.partial(kernel, n, mask),
        out_shape=jax.ShapeDtypeStruct((ROWS, QH * D), b16),
        in_specs=[sm, hbm, hbm, hbm, hbm, hbm],
        out_specs=vm,
        scratch_shapes=[
            pltpu.VMEM((ROWS, KVH * D), b16),
            pltpu.VMEM((ROWS, KVH * D), b16),
            pltpu.VMEM((ROWS, QH * D), b16),
            pltpu.VMEM((1, ROWS), i32),
            pltpu.VMEM((1, D), f32),
            pltpu.VMEM((KVH, 2, ROWS, D), b16),
            pltpu.VMEM((8, D), i32),
            pltpu.VMEM((KVH, QROWS, D), b16),
            pltpu.VMEM((KVH, n, 2, ROWS, D), b16),
            pltpu.VMEM((n, 8, D), i32),
            pltpu.VMEM((KVH, QROWS, D), b16),
            pltpu.VMEM((ROWS, n * ROWS), f32),
            pltpu.VMEM((KVH, QROWS, D), f32),
            pltpu.VMEM((KVH, QROWS, D), f32),
            pltpu.VMEM((KVH, QROWS, D), f32),
            dma((5,)),
            dma((2, KVH, half)), dma((KVH, n)),
            dma((KVH, 3)), dma((KVH,)),
            dma((2, half)), dma((n,)),
            dma((3,)), dma((1,)),
            dma((KVH,)), dma((KVH,)),
        ],
        compiler_params=pltpu.CompilerParams(
            collective_id=mask, has_side_effects=True, vmem_limit_bytes=56 * 1024 * 1024),
        name="gather_attend",
    )(*operands)


def on_device(queries, keys, values, positions, piece_lengths, dest_group, dest_offset):
    n = lax.axis_size("sp")
    groups = lax.axis_size("dp")
    mask = dest_group[0, 0] ^ lax.axis_index("dp")
    return lax.switch(
        mask, [functools.partial(attend, m, n) for m in range(groups)],
        piece_lengths.reshape(1), queries, keys, values, positions.reshape(1, ROWS),
        jnp.asarray(frequencies()))


def solution(mesh):
    in_specs = (
        P(("dp", "sp"), None), P(("dp", "sp"), None), P(("dp", "sp"), None), P(("dp", "sp")),
        P("dp", "sp", None), P("dp", None), P("dp", "sp", None),
    )
    return jax.shard_map(on_device, mesh=mesh, in_specs=in_specs,
                         out_specs=P(("dp", "sp"), None), check_vma=False)
```

```python
import functools

import jax
import jax.numpy as jnp
import numpy as np
from jax import lax
from jax.experimental import pallas as pl
from jax.experimental.pallas import tpu as pltpu
from jax.sharding import PartitionSpec as P

QH = 32
KVH = 8
D = 128
ROWS = 64
REP = QH // KVH
QROWS = REP * ROWS
THETA = 1000000.0
NEG = -1.0e30
FAR = 1 << 30
DIRECT = 4
SCALE = float(D ** -0.5 * np.log2(np.e))
MESH = pl.DeviceIdType.MESH


def frequencies():
    half = THETA ** (-(np.arange(D // 2, dtype=np.float64) * 2.0 / D))
    return np.concatenate([half, half])[None, :].astype(np.float32)


def kernel(n, mask, len_ref, q_ref, k_ref, v_ref, pos_ref, freq_ref, out_ref,
           kraw, vraw, qraw, praw, fraw, src, kpsrc, qsrc, kv, kp, rq, cap, o1, m1, l1,
           load, ksend, krecv, own_send, own_recv, psend, precv, pown_send, pown_recv, qsend, qrecv):
    z = lax.axis_index("sp")
    dp = lax.axis_index("dp")
    far = dp
    for bit in range(5):
        if mask >> bit & 1:
            far = far + (1 << bit) * (1 - 2 * lax.rem(lax.div(dp, 1 << bit), 2))
    right, left = lax.rem(z + 1, n), lax.rem(z + n - 1, n)
    half = n // 2
    OWN = half - 2
    FIRST = 3 * n // 4

    loads = [
        pltpu.make_async_copy(pos_ref, praw, load.at[0]),
        pltpu.make_async_copy(freq_ref, fraw, load.at[1]),
        pltpu.make_async_copy(k_ref, kraw, load.at[2]),
        pltpu.make_async_copy(v_ref, vraw, load.at[3]),
        pltpu.make_async_copy(q_ref, qraw, load.at[4]),
    ]
    for c in loads:
        c.start()
    peers = [(dp, left), (dp, right)]
    if mask:
        peers += [(far, z), (far, left), (far, right)]
    barrier = pltpu.get_barrier_semaphore()
    for peer in peers:
        pl.semaphore_signal(barrier, inc=1, device_id=peer, device_id_type=MESH)

    length = len_ref[0]
    rows = lax.broadcasted_iota(jnp.int32, (ROWS, D), 0)
    lanes = lax.broadcasted_iota(jnp.int32, (ROWS, D), 1)
    diag = rows == lax.rem(lanes, ROWS)
    live = rows < length
    loads[0].wait()
    loads[1].wait()
    pos_wide = jnp.broadcast_to(jnp.concatenate([praw[...], praw[...]], axis=1), (ROWS, D))
    pos_col = jnp.sum(jnp.where(rows == lanes, pos_wide, 0), axis=1, keepdims=True)
    angle = pos_col.astype(jnp.float32) * fraw[...]
    cosine = jnp.cos(angle)
    sine = jnp.sin(angle)
    sine = jnp.where(lanes < D // 2, -sine, sine)

    def rotate(x):
        x = x.astype(jnp.float32)
        return x * cosine + pltpu.roll(x, D // 2, 1) * sine

    key_pos = jnp.min(jnp.where(diag & live, pos_col, FAR), axis=0, keepdims=True)
    key_pos = jnp.broadcast_to(key_pos, (8, D))
    if mask:
        kpsrc[...] = key_pos
    else:
        kp[OWN] = key_pos
    loads[2].wait()
    loads[3].wait()
    for h in range(KVH):
        cols = pl.ds(h * D, D)
        rk = jnp.where(live, rotate(kraw[:, cols]), 0.0).astype(jnp.bfloat16)
        if mask:
            src[h, 0] = rk
            src[h, 1] = vraw[:, cols]
        else:
            kv[h, OWN, 0] = rk
            kv[h, OWN, 1] = vraw[:, cols]

    def slot(s):
        return lax.rem(s + OWN, n)

    def reach(h):
        return (half, n - 1 - half) if h % 2 == 0 else (n - 1 - half, half)

    def remote(a, b, s, r, device):
        return pltpu.make_async_remote_copy(
            src_ref=a, dst_ref=b, send_sem=s, recv_sem=r, device_id=device, device_id_type=MESH)

    def at(d, to_right):
        return slot(d) if to_right else slot(n - d)

    def copy(h, d, to_right):
        a, b = at(d, to_right), at(d + 1, to_right)
        return remote(kv.at[h, a], kv.at[h, b], ksend.at[0 if to_right else 1, h, d],
                      krecv.at[h, b], (dp, right if to_right else left))

    def pcopy(d, to_right):
        a, b = at(d, to_right), at(d + 1, to_right)
        return remote(kp.at[a], kp.at[b], psend.at[0 if to_right else 1, d],
                      precv.at[b], (dp, right if to_right else left))

    def own(h):
        return remote(src.at[h], kv.at[h, OWN], own_send.at[h, 0], own_recv.at[h], (far, z))

    def direct(h, to_right):
        b = at(1, to_right)
        return remote(src.at[h], kv.at[h, b], own_send.at[h, 1 if to_right else 2],
                      krecv.at[h, b], (far, right if to_right else left))

    def pown():
        return remote(kpsrc, kp.at[OWN], pown_send.at[0], pown_recv.at[0], (far, z))

    def pdirect(to_right):
        b = at(1, to_right)
        return remote(kpsrc, kp.at[b], pown_send.at[1 if to_right else 2],
                      precv.at[b], (far, right if to_right else left))

    def qcopy(h):
        return remote(qsrc.at[h], rq.at[h], qsend.at[h], qrecv.at[h], (far, z))

    pl.semaphore_wait(barrier, len(peers))

    BOTH = (True, False)
    straight = DIRECT if mask else 0
    if mask:
        for h in range(straight):
            direct(h, True).start()
            direct(h, False).start()
            if h == 0:
                for h2 in range(straight, KVH):
                    own(h2).start()
        for r in BOTH:
            pdirect(r).start()
        pown().start()
        for h in range(straight):
            own(h).start()
    else:
        for r in BOTH:
            pcopy(0, r).start()
    for h in range(straight, KVH):
        if mask:
            own(h).wait_recv()
        for r in BOTH:
            copy(h, 0, r).start()

    def step(d):
        for r in BOTH:
            pcopy(d - 1, r).wait_recv()
            pcopy(d, r).start()
        for h in range(KVH):
            for r in BOTH:
                copy(h, d - 1, r).wait_recv()
                copy(h, d, r).start()

    loads[4].wait()

    def early(d, _):
        step(d)
        for e in range(2):
            h = (d - 1) * 2 + e
            for g in range(REP):
                cols = pl.ds(pl.multiple_of((h * REP + g) * D, D), D)
                x = rotate(qraw[:, cols]).astype(jnp.bfloat16)
                if mask:
                    qsrc[h, g * ROWS:(g + 1) * ROWS] = x
                else:
                    rq[h, g * ROWS:(g + 1) * ROWS] = x
            if mask:
                qcopy(h).start()
        return 0

    lax.fori_loop(1, 5, early, 0)

    def middle(d, _):
        step(d)
        return 0

    lax.fori_loop(5, half - 2, middle, 0)

    if mask:
        pown().wait_recv()
        for h in range(straight):
            own(h).wait_recv()
    q_row = kp[OWN][0:1]
    q_col = jnp.min(jnp.where(rows == lanes, jnp.broadcast_to(q_row, (ROWS, D)), FAR),
                    axis=1, keepdims=True)
    q_live = q_col < FAR

    def build_cap(first, last):
        for t in range(first // 2, last // 2):
            pair = jnp.where(lanes[0:1] < ROWS, kp[2 * t, 0:1], kp[2 * t + 1, 0:1])
            cap[:, t * D:(t + 1) * D] = jnp.where(
                jnp.broadcast_to(pair, (ROWS, D)) <= q_col, jnp.float32(jnp.inf), NEG)

    def scores(h, first, last):
        keys = kv[h, first:last, 0].reshape((last - first) * ROWS, D)
        s = lax.dot_general(rq[h], keys, (((1,), (1,)), ((), ())),
                            preferred_element_type=jnp.float32)
        c = cap[:, first * ROWS:last * ROWS]
        s = jnp.minimum(s, jnp.concatenate([c] * REP, axis=0))
        return s, jnp.max(s, axis=1, keepdims=True)

    def weigh(h, s, m, first, last):
        vals = kv[h, first:last, 1].reshape((last - first) * ROWS, D)
        w = jnp.exp2(s * SCALE - m * SCALE)
        return jnp.sum(w, axis=1, keepdims=True), jnp.dot(
            w.astype(jnp.bfloat16), vals, preferred_element_type=jnp.float32)

    def part_one(h):
        if mask:
            qcopy(h).wait_recv()
        s, m = scores(h, 0, FIRST)
        total, o = weigh(h, s, m, 0, FIRST)
        o1[h] = o
        m1[h] = jnp.broadcast_to(m, (QROWS, D))
        l1[h] = jnp.broadcast_to(total, (QROWS, D))

    def part_two(h):
        s, m = scores(h, FIRST, n)
        m = jnp.maximum(m, m1[h][:, 0:1])
        total, o = weigh(h, s, m, FIRST, n)
        a = jnp.exp2((m1[h] - m) * SCALE)
        o = (o1[h] * a + o) / (l1[h] * a + total)
        parts = [jnp.where(q_live, o[g * ROWS:(g + 1) * ROWS], 0.0) for g in range(REP)]
        out_ref[:, pl.ds(pl.multiple_of(h * REP * D, D), REP * D)] = jnp.concatenate(
            parts, axis=1).astype(jnp.bfloat16)

    d = half - 2
    for r in BOTH:
        pcopy(d - 1, r).wait_recv()
        pcopy(d, r).start()
    build_cap(0, FIRST)

    def six(j, _):
        for e in range(2):
            h = 2 * j + e
            for r in BOTH:
                copy(h, d - 1, r).wait_recv()
                copy(h, d, r).start()
        part_one(j)
        return 0

    lax.fori_loop(0, KVH // 2, six, 0)
    for r in BOTH:
        pcopy(d, r).wait_recv()
    pcopy(d + 1, True).start()

    def seven(j, _):
        for e in range(2):
            h = 2 * j + e
            for r in BOTH:
                copy(h, d, r).wait_recv()
            copy(h, d + 1, e == 0).start()
        part_one(KVH // 2 + j)
        return 0

    lax.fori_loop(0, KVH // 2, seven, 0)
    pcopy(d + 1, True).wait_recv()
    build_cap(FIRST, n)

    def eight(j, _):
        for e in range(2):
            h = 2 * j + e
            copy(h, d + 1, e == 0).wait_recv()
            part_two(h)
        return 0

    lax.fori_loop(0, KVH // 2, eight, 0)

    if mask:
        for r in BOTH:
            pdirect(r).wait_send()
        pown().wait_send()
        for h in range(KVH):
            own(h).wait_send()
            qcopy(h).wait_send()
        for h in range(straight):
            for r in BOTH:
                direct(h, r).wait_send()
    else:
        for r in BOTH:
            pcopy(0, r).wait_send()
    for h in range(straight, KVH):
        for r in BOTH:
            copy(h, 0, r).wait_send()

    def drain(d, _):
        for r in BOTH:
            pcopy(d, r).wait_send()
            for h in range(KVH):
                copy(h, d, r).wait_send()
        return 0

    lax.fori_loop(1, half - 1, drain, 0)
    pcopy(half - 1, True).wait_send()
    for h in range(KVH):
        copy(h, half - 1, h % 2 == 0).wait_send()


def attend(mask, n, *operands):
    vm = pl.BlockSpec(memory_space=pltpu.VMEM)
    sm = pl.BlockSpec(memory_space=pltpu.SMEM)
    hbm = pl.BlockSpec(memory_space=pl.ANY)
    dma = pltpu.SemaphoreType.DMA
    b16, f32, i32 = jnp.bfloat16, jnp.float32, jnp.int32
    half = n // 2
    return pl.pallas_call(
        functools.partial(kernel, n, mask),
        out_shape=jax.ShapeDtypeStruct((ROWS, QH * D), b16),
        in_specs=[sm, hbm, hbm, hbm, hbm, hbm],
        out_specs=vm,
        scratch_shapes=[
            pltpu.VMEM((ROWS, KVH * D), b16),
            pltpu.VMEM((ROWS, KVH * D), b16),
            pltpu.VMEM((ROWS, QH * D), b16),
            pltpu.VMEM((1, ROWS), i32),
            pltpu.VMEM((1, D), f32),
            pltpu.VMEM((KVH, 2, ROWS, D), b16),
            pltpu.VMEM((8, D), i32),
            pltpu.VMEM((KVH, QROWS, D), b16),
            pltpu.VMEM((KVH, n, 2, ROWS, D), b16),
            pltpu.VMEM((n, 8, D), i32),
            pltpu.VMEM((KVH, QROWS, D), b16),
            pltpu.VMEM((ROWS, n * ROWS), f32),
            pltpu.VMEM((KVH, QROWS, D), f32),
            pltpu.VMEM((KVH, QROWS, D), f32),
            pltpu.VMEM((KVH, QROWS, D), f32),
            dma((5,)),
            dma((2, KVH, half)), dma((KVH, n)),
            dma((KVH, 3)), dma((KVH,)),
            dma((2, half)), dma((n,)),
            dma((3,)), dma((1,)),
            dma((KVH,)), dma((KVH,)),
        ],
        compiler_params=pltpu.CompilerParams(
            collective_id=mask, has_side_effects=True, vmem_limit_bytes=56 * 1024 * 1024),
        name="gather_attend",
    )(*operands)


def on_device(queries, keys, values, positions, piece_lengths, dest_group, dest_offset):
    n = lax.axis_size("sp")
    groups = lax.axis_size("dp")
    mask = dest_group[0, 0] ^ lax.axis_index("dp")
    out = attend(0, n, piece_lengths.reshape(1), queries, keys, values,
                 positions.reshape(1, ROWS), jnp.asarray(frequencies()))
    return lax.switch(mask, [
        functools.partial(lambda m, x: lax.ppermute(x, "dp", [(i, i ^ m) for i in range(groups)]), m)
        for m in range(groups)
    ], out)


def solution(mesh):
    in_specs = (
        P(("dp", "sp"), None), P(("dp", "sp"), None), P(("dp", "sp"), None), P(("dp", "sp")),
        P("dp", "sp", None), P("dp", None), P("dp", "sp", None),
    )
    return jax.shard_map(on_device, mesh=mesh, in_specs=in_specs,
                         out_specs=P(("dp", "sp"), None), check_vma=False)
```

```python
import functools

import jax
import jax.numpy as jnp
import numpy as np
from jax import lax
from jax.experimental import pallas as pl
from jax.experimental.pallas import tpu as pltpu
from jax.sharding import PartitionSpec as P

QH = 32
KVH = 8
D = 128
ROWS = 64
REP = QH // KVH
QROWS = REP * ROWS
THETA = 1000000.0
NEG = -1.0e30
FAR = 1 << 30
SCALE = float(D ** -0.5 * np.log2(np.e))
MESH = pl.DeviceIdType.MESH


def frequencies():
    half = THETA ** (-(np.arange(D // 2, dtype=np.float64) * 2.0 / D))
    return np.concatenate([half, half])[None, :].astype(np.float32)


def kernel(n, len_ref, q_ref, k_ref, v_ref, pos_ref, freq_ref, out_ref,
           lraw, kraw, vraw, qraw, praw, fraw, kv, kp, rq, cap, o1, m1, l1,
           load, ksend, krecv, vsend, vrecv, psend, precv):
    z = lax.axis_index("sp")
    dp = lax.axis_index("dp")
    right, left = lax.rem(z + 1, n), lax.rem(z + n - 1, n)
    half = n // 2
    OWN = half - 2
    FIRST = 3 * n // 4

    loads = [
        pltpu.make_async_copy(pos_ref, praw, load.at[0]),
        pltpu.make_async_copy(freq_ref, fraw, load.at[1]),
        pltpu.make_async_copy(k_ref, kraw, load.at[2]),
        pltpu.make_async_copy(v_ref, vraw, load.at[3]),
        pltpu.make_async_copy(q_ref, qraw, load.at[4]),
        pltpu.make_async_copy(len_ref, lraw, load.at[5]),
    ]
    for c in loads:
        c.start()
    peers = [(dp, left), (dp, right)]
    barrier = pltpu.get_barrier_semaphore()
    for peer in peers:
        pl.semaphore_signal(barrier, inc=1, device_id=peer, device_id_type=MESH)

    rows = lax.broadcasted_iota(jnp.int32, (ROWS, D), 0)
    lanes = lax.broadcasted_iota(jnp.int32, (ROWS, D), 1)
    diag = rows == lax.rem(lanes, ROWS)
    def slot(s):
        return lax.rem(s + OWN, n)

    def reach(h):
        return (half, n - 1 - half) if h % 2 == 0 else (n - 1 - half, half)

    def remote(a, b, s, r, device):
        return pltpu.make_async_remote_copy(
            src_ref=a, dst_ref=b, send_sem=s, recv_sem=r, device_id=device, device_id_type=MESH)

    def at(d, to_right):
        return slot(d) if to_right else slot(n - d)

    def copy(h, d, to_right):
        a, b = at(d, to_right), at(d + 1, to_right)
        return remote(kv.at[h, a], kv.at[h, b], ksend.at[0 if to_right else 1, h, d],
                      krecv.at[h, b], (dp, right if to_right else left))

    def pcopy(d, to_right):
        a, b = at(d, to_right), at(d + 1, to_right)
        return remote(kp.at[a], kp.at[b], psend.at[0 if to_right else 1, d],
                      precv.at[b], (dp, right if to_right else left))

    def vcopy(h, to_right):
        a, b = at(0, to_right), at(1, to_right)
        side = 0 if to_right else 1
        return remote(kv.at[h, a, 1], kv.at[h, b, 1], vsend.at[side, h], vrecv.at[side, h],
                      (dp, right if to_right else left))

    def kcopy(h, to_right):
        a, b = at(0, to_right), at(1, to_right)
        return remote(kv.at[h, a, 0], kv.at[h, b, 0], ksend.at[0 if to_right else 1, h, 0],
                      krecv.at[h, b], (dp, right if to_right else left))

    BOTH = (True, False)
    loads[3].wait()
    for h in range(KVH):
        kv[h, OWN, 1] = vraw[:, h * D:(h + 1) * D]
    pl.semaphore_wait(barrier, len(peers))
    for h in range(KVH):
        for r in BOTH:
            vcopy(h, r).start()

    for i in (5, 0, 1):
        loads[i].wait()
    live = rows < lraw[0, 0, 0]
    pos_wide = jnp.broadcast_to(jnp.concatenate([praw[...], praw[...]], axis=1), (ROWS, D))
    pos_col = jnp.sum(jnp.where(rows == lanes, pos_wide, 0), axis=1, keepdims=True)
    angle = pos_col.astype(jnp.float32) * fraw[...]
    cosine = jnp.cos(angle)
    sine = jnp.sin(angle)
    sine = jnp.where(lanes < D // 2, -sine, sine)

    def rotate(x):
        x = x.astype(jnp.float32)
        return x * cosine + pltpu.roll(x, D // 2, 1) * sine

    loads[2].wait()
    for h in range(KVH):
        rk = jnp.where(live, rotate(kraw[:, h * D:(h + 1) * D]), 0.0)
        kv[h, OWN, 0] = rk.astype(jnp.bfloat16)
        for r in BOTH:
            kcopy(h, r).start()
    key_pos = jnp.min(jnp.where(diag & live, pos_col, FAR), axis=0, keepdims=True)
    kp[OWN] = jnp.broadcast_to(key_pos, (8, D))
    for r in BOTH:
        pcopy(0, r).start()

    def step(d):
        for r in BOTH:
            pcopy(d - 1, r).wait_recv()
            pcopy(d, r).start()
        for h in range(KVH):
            for r in BOTH:
                copy(h, d - 1, r).wait_recv()
                copy(h, d, r).start()

    for h in range(KVH):
        for r in BOTH:
            vcopy(h, r).wait_recv()
            kcopy(h, r).wait_recv()
            copy(h, 1, r).start()
    for r in BOTH:
        pcopy(0, r).wait_recv()
        pcopy(1, r).start()
    loads[4].wait()

    def rotate_q(h):
        for g in range(REP):
            cols = pl.ds(pl.multiple_of((h * REP + g) * D, D), D)
            rq[h, g * ROWS:(g + 1) * ROWS] = rotate(qraw[:, cols]).astype(jnp.bfloat16)

    def early(d, _):
        for e in range(2):
            rotate_q((d - 2) * 2 + e)
        step(d)
        return 0

    lax.fori_loop(2, half - 2, early, 0)

    q_row = kp[OWN][0:1]
    q_col = jnp.min(jnp.where(rows == lanes, jnp.broadcast_to(q_row, (ROWS, D)), FAR),
                    axis=1, keepdims=True)
    q_live = q_col < FAR

    def build_cap(first, last):
        for t in range(first // 2, last // 2):
            pair = jnp.where(lanes[0:1] < ROWS, kp[2 * t, 0:1], kp[2 * t + 1, 0:1])
            cap[:, t * D:(t + 1) * D] = jnp.where(
                jnp.broadcast_to(pair, (ROWS, D)) <= q_col, jnp.float32(jnp.inf), NEG)

    def scores(h, first, last):
        keys = kv[h, first:last, 0].reshape((last - first) * ROWS, D)
        s = lax.dot_general(rq[h], keys, (((1,), (1,)), ((), ())),
                            preferred_element_type=jnp.float32)
        c = cap[:, first * ROWS:last * ROWS]
        s = jnp.minimum(s, jnp.concatenate([c] * REP, axis=0))
        return s, jnp.max(s, axis=1, keepdims=True)

    def weigh(h, s, m, first, last):
        vals = kv[h, first:last, 1].reshape((last - first) * ROWS, D)
        w = jnp.exp2(s * SCALE - m * SCALE)
        return jnp.sum(w, axis=1, keepdims=True), jnp.dot(
            w.astype(jnp.bfloat16), vals, preferred_element_type=jnp.float32)

    def part_one(h):
        s, m = scores(h, 0, FIRST)
        total, o = weigh(h, s, m, 0, FIRST)
        o1[h] = o
        m1[h] = jnp.broadcast_to(m, (QROWS, D))
        l1[h] = jnp.broadcast_to(total, (QROWS, D))

    def part_two(h):
        s, m = scores(h, FIRST, n)
        m = jnp.maximum(m, m1[h][:, 0:1])
        total, o = weigh(h, s, m, FIRST, n)
        a = jnp.exp2((m1[h] - m) * SCALE)
        o = (o1[h] * a + o) / (l1[h] * a + total)
        parts = [jnp.where(q_live, o[g * ROWS:(g + 1) * ROWS], 0.0) for g in range(REP)]
        out_ref[:, pl.ds(pl.multiple_of(h * REP * D, D), REP * D)] = jnp.concatenate(
            parts, axis=1).astype(jnp.bfloat16)

    d = half - 2
    for r in BOTH:
        pcopy(d - 1, r).wait_recv()
        pcopy(d, r).start()
    build_cap(0, FIRST)

    def six(j, _):
        for e in range(2):
            h = 2 * j + e
            for r in BOTH:
                copy(h, d - 1, r).wait_recv()
                copy(h, d, r).start()
        part_one(j)
        return 0

    lax.fori_loop(0, KVH // 2, six, 0)
    for r in BOTH:
        pcopy(d, r).wait_recv()
    pcopy(d + 1, True).start()

    def seven(j, _):
        for e in range(2):
            h = 2 * j + e
            for r in BOTH:
                copy(h, d, r).wait_recv()
            copy(h, d + 1, e == 0).start()
        part_one(KVH // 2 + j)
        return 0

    lax.fori_loop(0, KVH // 2, seven, 0)
    pcopy(d + 1, True).wait_recv()
    build_cap(FIRST, n)

    def eight(j, _):
        for e in range(2):
            h = 2 * j + e
            copy(h, d + 1, e == 0).wait_recv()
            part_two(h)
        return 0

    lax.fori_loop(0, KVH // 2, eight, 0)

    for r in BOTH:
        pcopy(0, r).wait_send()
        for h in range(KVH):
            vcopy(h, r).wait_send()
            kcopy(h, r).wait_send()

    def drain(d, _):
        for r in BOTH:
            pcopy(d, r).wait_send()
            for h in range(KVH):
                copy(h, d, r).wait_send()
        return 0

    lax.fori_loop(1, half - 1, drain, 0)
    pcopy(half - 1, True).wait_send()
    for h in range(KVH):
        copy(h, half - 1, h % 2 == 0).wait_send()


def attend(n, *operands):
    vm = pl.BlockSpec(memory_space=pltpu.VMEM)
    hbm = pl.BlockSpec(memory_space=pl.ANY)
    dma = pltpu.SemaphoreType.DMA
    b16, f32, i32 = jnp.bfloat16, jnp.float32, jnp.int32
    half = n // 2
    return pl.pallas_call(
        functools.partial(kernel, n),
        out_shape=jax.ShapeDtypeStruct((ROWS, QH * D), b16),
        in_specs=[hbm, hbm, hbm, hbm, hbm, hbm],
        out_specs=vm,
        scratch_shapes=[
            pltpu.SMEM((1, 1, 1), i32),
            pltpu.VMEM((ROWS, KVH * D), b16),
            pltpu.VMEM((ROWS, KVH * D), b16),
            pltpu.VMEM((ROWS, QH * D), b16),
            pltpu.VMEM((1, ROWS), i32),
            pltpu.VMEM((1, D), f32),
            pltpu.VMEM((KVH, n, 2, ROWS, D), b16),
            pltpu.VMEM((n, 8, D), i32),
            pltpu.VMEM((KVH, QROWS, D), b16),
            pltpu.VMEM((ROWS, n * ROWS), f32),
            pltpu.VMEM((KVH, QROWS, D), f32),
            pltpu.VMEM((KVH, QROWS, D), f32),
            pltpu.VMEM((KVH, QROWS, D), f32),
            dma((6,)),
            dma((2, KVH, half)), dma((KVH, n)),
            dma((2, KVH)), dma((2, KVH)),
            dma((2, half)), dma((n,)),
        ],
        compiler_params=pltpu.CompilerParams(
            collective_id=0, has_side_effects=True, vmem_limit_bytes=56 * 1024 * 1024),
        name="gather_attend",
    )(*operands)


def place_kernel(x_ref, out_ref, done):
    copies = []
    for p in range(8):
        part = (pl.ds(p // 2 * 16, 16), pl.ds(p % 2 * (QH * D // 2), QH * D // 2))
        copies.append(pltpu.make_async_copy(x_ref.at[part], out_ref.at[part], done.at[p]))
    for c in copies:
        c.start()
    for c in copies:
        c.wait()


def place(x):
    hbm = pl.BlockSpec(memory_space=pl.ANY)
    return pl.pallas_call(
        place_kernel, out_shape=jax.ShapeDtypeStruct(x.shape, x.dtype), in_specs=[hbm],
        out_specs=hbm, scratch_shapes=[pltpu.SemaphoreType.DMA((8,))], name="place",
    )(x)


def on_device(queries, keys, values, positions, piece_lengths, dest_group, dest_offset):
    n = lax.axis_size("sp")
    groups = lax.axis_size("dp")
    mask = dest_group[0, 0] ^ lax.axis_index("dp")
    out = attend(n, piece_lengths, queries, keys, values,
                 positions.reshape(1, ROWS), jnp.asarray(frequencies()))
    return place(lax.switch(mask, [
        functools.partial(lambda m, x: lax.ppermute(x, "dp", [(i, i ^ m) for i in range(groups)]), m)
        for m in range(groups)
    ], out))


def solution(mesh):
    in_specs = (
        P(("dp", "sp"), None), P(("dp", "sp"), None), P(("dp", "sp"), None), P(("dp", "sp")),
        P("dp", "sp", None), P("dp", None), P("dp", "sp", None),
    )
    return jax.shard_map(on_device, mesh=mesh, in_specs=in_specs,
                         out_specs=P(("dp", "sp"), None), check_vma=False)
```

```python
import functools

import jax
import jax.numpy as jnp
import numpy as np
from jax import lax
from jax.experimental import pallas as pl
from jax.experimental.pallas import tpu as pltpu
from jax.sharding import PartitionSpec as P

QH = 32
KVH = 8
D = 128
ROWS = 64
REP = QH // KVH
QROWS = REP * ROWS
THETA = 1000000.0
NEG = -1.0e30
FAR = 1 << 30
SCALE = float(D ** -0.5 * np.log2(np.e))
MESH = pl.DeviceIdType.MESH


def frequencies():
    half = THETA ** (-(np.arange(D // 2, dtype=np.float64) * 2.0 / D))
    return np.concatenate([half, half])[None, :].astype(np.float32)


def kernel(n, len_ref, q_ref, k_ref, v_ref, pos_ref, freq_ref, out_ref,
           lraw, kraw, vraw, qraw, praw, fraw, kv, kp, rq, cap, o1, m1, l1,
           load, ksend, krecv, vsend, vrecv, psend, precv):
    z = lax.axis_index("sp")
    dp = lax.axis_index("dp")
    right, left = lax.rem(z + 1, n), lax.rem(z + n - 1, n)
    half = n // 2
    OWN = half - 2
    FIRST = 3 * n // 4

    loads = [
        pltpu.make_async_copy(pos_ref, praw, load.at[0]),
        pltpu.make_async_copy(freq_ref, fraw, load.at[1]),
        pltpu.make_async_copy(k_ref, kraw, load.at[2]),
        pltpu.make_async_copy(v_ref, vraw, load.at[3]),
        pltpu.make_async_copy(q_ref, qraw, load.at[4]),
        pltpu.make_async_copy(len_ref, lraw, load.at[5]),
    ]
    for c in loads:
        c.start()
    peers = [(dp, left), (dp, right)]
    barrier = pltpu.get_barrier_semaphore()
    for peer in peers:
        pl.semaphore_signal(barrier, inc=1, device_id=peer, device_id_type=MESH)

    rows = lax.broadcasted_iota(jnp.int32, (ROWS, D), 0)
    lanes = lax.broadcasted_iota(jnp.int32, (ROWS, D), 1)
    diag = rows == lax.rem(lanes, ROWS)
    def slot(s):
        return lax.rem(s + OWN, n)

    def reach(h):
        return (half, n - 1 - half) if h % 2 == 0 else (n - 1 - half, half)

    def remote(a, b, s, r, device):
        return pltpu.make_async_remote_copy(
            src_ref=a, dst_ref=b, send_sem=s, recv_sem=r, device_id=device, device_id_type=MESH)

    def at(d, to_right):
        return slot(d) if to_right else slot(n - d)

    def copy(h, d, to_right):
        a, b = at(d, to_right), at(d + 1, to_right)
        return remote(kv.at[h, a], kv.at[h, b], ksend.at[0 if to_right else 1, h, d],
                      krecv.at[h, b], (dp, right if to_right else left))

    def pcopy(d, to_right):
        a, b = at(d, to_right), at(d + 1, to_right)
        return remote(kp.at[a], kp.at[b], psend.at[0 if to_right else 1, d],
                      precv.at[b], (dp, right if to_right else left))

    def vcopy(h, to_right):
        a, b = at(0, to_right), at(1, to_right)
        side = 0 if to_right else 1
        return remote(kv.at[h, a, 1], kv.at[h, b, 1], vsend.at[side, h], vrecv.at[side, h],
                      (dp, right if to_right else left))

    def kcopy(h, to_right):
        a, b = at(0, to_right), at(1, to_right)
        return remote(kv.at[h, a, 0], kv.at[h, b, 0], ksend.at[0 if to_right else 1, h, 0],
                      krecv.at[h, b], (dp, right if to_right else left))

    BOTH = (True, False)
    loads[3].wait()
    for h in range(KVH):
        kv[h, OWN, 1] = vraw[:, h * D:(h + 1) * D]
    pl.semaphore_wait(barrier, len(peers))
    for h in range(KVH):
        for r in BOTH:
            vcopy(h, r).start()

    for i in (5, 0, 1):
        loads[i].wait()
    live = rows < lraw[0, 0, 0]
    pos_wide = jnp.broadcast_to(jnp.concatenate([praw[...], praw[...]], axis=1), (ROWS, D))
    pos_col = jnp.sum(jnp.where(rows == lanes, pos_wide, 0), axis=1, keepdims=True)
    angle = pos_col.astype(jnp.float32) * fraw[...]
    cosine = jnp.cos(angle)
    sine = jnp.sin(angle)
    sine = jnp.where(lanes < D // 2, -sine, sine)

    def rotate(x):
        x = x.astype(jnp.float32)
        return x * cosine + pltpu.roll(x, D // 2, 1) * sine

    loads[2].wait()
    for h in range(KVH):
        rk = jnp.where(live, rotate(kraw[:, h * D:(h + 1) * D]), 0.0)
        kv[h, OWN, 0] = rk.astype(jnp.bfloat16)
        for r in BOTH:
            kcopy(h, r).start()
    key_pos = jnp.min(jnp.where(diag & live, pos_col, FAR), axis=0, keepdims=True)
    kp[OWN] = jnp.broadcast_to(key_pos, (8, D))
    for r in BOTH:
        pcopy(0, r).start()

    def step(d):
        for r in BOTH:
            pcopy(d - 1, r).wait_recv()
            pcopy(d, r).start()
        for h in range(KVH):
            for r in BOTH:
                copy(h, d - 1, r).wait_recv()
                copy(h, d, r).start()

    for h in range(KVH):
        for r in BOTH:
            vcopy(h, r).wait_recv()
            kcopy(h, r).wait_recv()
            copy(h, 1, r).start()
    for r in BOTH:
        pcopy(0, r).wait_recv()
        pcopy(1, r).start()
    loads[4].wait()

    def rotate_q(h):
        for g in range(REP):
            cols = pl.ds(pl.multiple_of((h * REP + g) * D, D), D)
            rq[h, g * ROWS:(g + 1) * ROWS] = rotate(qraw[:, cols]).astype(jnp.bfloat16)

    def early(d, _):
        for e in range(2):
            rotate_q((d - 2) * 2 + e)
        step(d)
        return 0

    lax.fori_loop(2, half - 2, early, 0)

    q_row = kp[OWN][0:1]
    q_col = jnp.min(jnp.where(rows == lanes, jnp.broadcast_to(q_row, (ROWS, D)), FAR),
                    axis=1, keepdims=True)
    q_live = q_col < FAR

    def build_cap(first, last):
        for t in range(first // 2, last // 2):
            pair = jnp.where(lanes[0:1] < ROWS, kp[2 * t, 0:1], kp[2 * t + 1, 0:1])
            cap[:, t * D:(t + 1) * D] = jnp.where(
                jnp.broadcast_to(pair, (ROWS, D)) <= q_col, jnp.float32(jnp.inf), NEG)

    def scores(h, first, last):
        keys = kv[h, first:last, 0].reshape((last - first) * ROWS, D)
        s = lax.dot_general(rq[h], keys, (((1,), (1,)), ((), ())),
                            preferred_element_type=jnp.float32)
        c = cap[:, first * ROWS:last * ROWS]
        s = jnp.minimum(s, jnp.concatenate([c] * REP, axis=0))
        return s, jnp.max(s, axis=1, keepdims=True)

    def weigh(h, s, m, first, last):
        vals = kv[h, first:last, 1].reshape((last - first) * ROWS, D)
        w = jnp.exp2(s * SCALE - m * SCALE)
        return jnp.sum(w, axis=1, keepdims=True), jnp.dot(
            w.astype(jnp.bfloat16), vals, preferred_element_type=jnp.float32)

    def part_one(h):
        s, m = scores(h, 0, FIRST)
        total, o = weigh(h, s, m, 0, FIRST)
        o1[h] = o
        m1[h] = jnp.broadcast_to(m, (QROWS, D))
        l1[h] = jnp.broadcast_to(total, (QROWS, D))

    def part_two(h):
        s, m = scores(h, FIRST, n)
        m = jnp.maximum(m, m1[h][:, 0:1])
        total, o = weigh(h, s, m, FIRST, n)
        a = jnp.exp2((m1[h] - m) * SCALE)
        o = (o1[h] * a + o) / (l1[h] * a + total)
        parts = [jnp.where(q_live, o[g * ROWS:(g + 1) * ROWS], 0.0) for g in range(REP)]
        out_ref[:, pl.ds(pl.multiple_of(h * REP * D, D), REP * D)] = jnp.concatenate(
            parts, axis=1).astype(jnp.bfloat16)

    d = half - 2
    for r in BOTH:
        pcopy(d - 1, r).wait_recv()
        pcopy(d, r).start()
    build_cap(0, FIRST)

    def six(j, _):
        for e in range(2):
            h = 2 * j + e
            for r in BOTH:
                copy(h, d - 1, r).wait_recv()
                copy(h, d, r).start()
        part_one(j)
        return 0

    lax.fori_loop(0, KVH // 2, six, 0)
    for r in BOTH:
        pcopy(d, r).wait_recv()
    pcopy(d + 1, True).start()

    def seven(j, _):
        for e in range(2):
            h = 2 * j + e
            for r in BOTH:
                copy(h, d, r).wait_recv()
            copy(h, d + 1, e == 0).start()
        part_one(KVH // 2 + j)
        return 0

    lax.fori_loop(0, KVH // 2, seven, 0)
    pcopy(d + 1, True).wait_recv()
    build_cap(FIRST, n)

    def eight(j, _):
        for e in range(2):
            h = 2 * j + e
            copy(h, d + 1, e == 0).wait_recv()
            part_two(h)
        return 0

    lax.fori_loop(0, KVH // 2, eight, 0)

    for r in BOTH:
        pcopy(0, r).wait_send()
        for h in range(KVH):
            vcopy(h, r).wait_send()
            kcopy(h, r).wait_send()

    def drain(d, _):
        for r in BOTH:
            pcopy(d, r).wait_send()
            for h in range(KVH):
                copy(h, d, r).wait_send()
        return 0

    lax.fori_loop(1, half - 1, drain, 0)
    pcopy(half - 1, True).wait_send()
    for h in range(KVH):
        copy(h, half - 1, h % 2 == 0).wait_send()


def attend(n, *operands):
    vm = pl.BlockSpec(memory_space=pltpu.VMEM)
    hbm = pl.BlockSpec(memory_space=pl.ANY)
    dma = pltpu.SemaphoreType.DMA
    b16, f32, i32 = jnp.bfloat16, jnp.float32, jnp.int32
    half = n // 2
    return pl.pallas_call(
        functools.partial(kernel, n),
        out_shape=jax.ShapeDtypeStruct((ROWS, QH * D), b16),
        in_specs=[hbm, hbm, hbm, hbm, hbm, hbm],
        out_specs=vm,
        scratch_shapes=[
            pltpu.SMEM((1, 1, 1), i32),
            pltpu.VMEM((ROWS, KVH * D), b16),
            pltpu.VMEM((ROWS, KVH * D), b16),
            pltpu.VMEM((ROWS, QH * D), b16),
            pltpu.VMEM((1, ROWS), i32),
            pltpu.VMEM((1, D), f32),
            pltpu.VMEM((KVH, n, 2, ROWS, D), b16),
            pltpu.VMEM((n, 8, D), i32),
            pltpu.VMEM((KVH, QROWS, D), b16),
            pltpu.VMEM((ROWS, n * ROWS), f32),
            pltpu.VMEM((KVH, QROWS, D), f32),
            pltpu.VMEM((KVH, QROWS, D), f32),
            pltpu.VMEM((KVH, QROWS, D), f32),
            dma((6,)),
            dma((2, KVH, half)), dma((KVH, n)),
            dma((2, KVH)), dma((2, KVH)),
            dma((2, half)), dma((n,)),
        ],
        compiler_params=pltpu.CompilerParams(
            collective_id=0, has_side_effects=True, vmem_limit_bytes=56 * 1024 * 1024),
        name="gather_attend",
    )(*operands)


def on_device(queries, keys, values, positions, piece_lengths, dest_group, dest_offset):
    n = lax.axis_size("sp")
    groups = lax.axis_size("dp")
    mask = dest_group[0, 0] ^ lax.axis_index("dp")
    out = attend(n, piece_lengths, queries, keys, values,
                 positions.reshape(1, ROWS), jnp.asarray(frequencies()))
    out = lax.switch(mask, [
        functools.partial(lambda m, x: lax.ppermute(x, "dp", [(i, i ^ m) for i in range(groups)]), m)
        for m in range(groups)
    ], out)
    named = (mask >= 0) & (mask < groups)
    return jnp.where(named, out, jnp.zeros_like(out))


def solution(mesh):
    in_specs = (
        P(("dp", "sp"), None), P(("dp", "sp"), None), P(("dp", "sp"), None), P(("dp", "sp")),
        P("dp", "sp", None), P("dp", None), P("dp", "sp", None),
    )
    return jax.shard_map(on_device, mesh=mesh, in_specs=in_specs,
                         out_specs=P(("dp", "sp"), None), check_vma=False)
```

```python
import functools

import jax
import jax.numpy as jnp
import numpy as np
from jax import lax
from jax.experimental import pallas as pl
from jax.experimental.pallas import tpu as pltpu
from jax.sharding import PartitionSpec as P

QH = 32
KVH = 8
D = 128
ROWS = 64
REP = QH // KVH
QROWS = REP * ROWS
THETA = 1000000.0
NEG = -1.0e30
FAR = 1 << 30
SCALE = float(D ** -0.5 * np.log2(np.e))
MESH = pl.DeviceIdType.MESH


def frequencies():
    half = THETA ** (-(np.arange(D // 2, dtype=np.float64) * 2.0 / D))
    return np.concatenate([half, half])[None, :].astype(np.float32)


def kernel(n, len_ref, q_ref, k_ref, v_ref, pos_ref, freq_ref, out_ref,
           lraw, kraw, vraw, qraw, praw, fraw, kv, kp, rq, cap, o1, m1, l1,
           load, ksend, krecv, vsend, vrecv, psend, precv):
    z = lax.axis_index("sp")
    dp = lax.axis_index("dp")
    right, left = lax.rem(z + 1, n), lax.rem(z + n - 1, n)
    half = n // 2
    OWN = half - 2
    FIRST = 3 * n // 4

    peers = [(dp, left), (dp, right)]
    barrier = pltpu.get_barrier_semaphore()
    for peer in peers:
        pl.semaphore_signal(barrier, inc=1, device_id=peer, device_id_type=MESH)

    loads = [
        pltpu.make_async_copy(pos_ref, praw, load.at[0]),
        pltpu.make_async_copy(freq_ref, fraw, load.at[1]),
        pltpu.make_async_copy(k_ref, kraw, load.at[2]),
        pltpu.make_async_copy(v_ref, vraw, load.at[3]),
        pltpu.make_async_copy(q_ref, qraw, load.at[4]),
        pltpu.make_async_copy(len_ref, lraw, load.at[5]),
    ]
    for i in (3, 5, 0, 1, 2, 4):
        loads[i].start()

    rows = lax.broadcasted_iota(jnp.int32, (ROWS, D), 0)
    lanes = lax.broadcasted_iota(jnp.int32, (ROWS, D), 1)
    diag = rows == lax.rem(lanes, ROWS)
    def slot(s):
        return lax.rem(s + OWN, n)

    def reach(h):
        return (half, n - 1 - half) if h % 2 == 0 else (n - 1 - half, half)

    def remote(a, b, s, r, device):
        return pltpu.make_async_remote_copy(
            src_ref=a, dst_ref=b, send_sem=s, recv_sem=r, device_id=device, device_id_type=MESH)

    def at(d, to_right):
        return slot(d) if to_right else slot(n - d)

    def copy(h, d, to_right):
        a, b = at(d, to_right), at(d + 1, to_right)
        return remote(kv.at[h, a], kv.at[h, b], ksend.at[0 if to_right else 1, h, d],
                      krecv.at[h, b], (dp, right if to_right else left))

    def pcopy(d, to_right):
        a, b = at(d, to_right), at(d + 1, to_right)
        return remote(kp.at[a], kp.at[b], psend.at[0 if to_right else 1, d],
                      precv.at[b], (dp, right if to_right else left))

    def vcopy(h, to_right):
        a, b = at(0, to_right), at(1, to_right)
        side = 0 if to_right else 1
        return remote(kv.at[h, a, 1], kv.at[h, b, 1], vsend.at[side, h], vrecv.at[side, h],
                      (dp, right if to_right else left))

    def kcopy(h, to_right):
        a, b = at(0, to_right), at(1, to_right)
        return remote(kv.at[h, a, 0], kv.at[h, b, 0], ksend.at[0 if to_right else 1, h, 0],
                      krecv.at[h, b], (dp, right if to_right else left))

    BOTH = (True, False)
    loads[3].wait()
    pl.semaphore_wait(barrier, len(peers))
    for h in range(KVH):
        kv[h, OWN, 1] = vraw[:, h * D:(h + 1) * D]
        for r in BOTH:
            vcopy(h, r).start()

    for i in (5, 0, 1):
        loads[i].wait()
    live = rows < lraw[0, 0, 0]
    pos_wide = jnp.broadcast_to(jnp.concatenate([praw[...], praw[...]], axis=1), (ROWS, D))
    pos_col = jnp.sum(jnp.where(rows == lanes, pos_wide, 0), axis=1, keepdims=True)
    angle = pos_col.astype(jnp.float32) * fraw[...]
    cosine = jnp.cos(angle)
    sine = jnp.sin(angle)
    sine = jnp.where(lanes < D // 2, -sine, sine)

    def rotate(x):
        x = x.astype(jnp.float32)
        return x * cosine + pltpu.roll(x, D // 2, 1) * sine

    loads[2].wait()
    for h in range(KVH):
        rk = jnp.where(live, rotate(kraw[:, h * D:(h + 1) * D]), 0.0)
        kv[h, OWN, 0] = rk.astype(jnp.bfloat16)
        for r in BOTH:
            kcopy(h, r).start()
    key_pos = jnp.min(jnp.where(diag & live, pos_col, FAR), axis=0, keepdims=True)
    kp[OWN] = jnp.broadcast_to(key_pos, (8, D))
    for r in BOTH:
        pcopy(0, r).start()

    def step(d):
        for r in BOTH:
            pcopy(d - 1, r).wait_recv()
            pcopy(d, r).start()
        for h in range(KVH):
            for r in BOTH:
                copy(h, d - 1, r).wait_recv()
                copy(h, d, r).start()

    for h in range(KVH):
        for r in BOTH:
            vcopy(h, r).wait_recv()
            kcopy(h, r).wait_recv()
            copy(h, 1, r).start()
    for r in BOTH:
        pcopy(0, r).wait_recv()
        pcopy(1, r).start()
    loads[4].wait()

    def rotate_q(h):
        for g in range(REP):
            cols = pl.ds(pl.multiple_of((h * REP + g) * D, D), D)
            rq[h, g * ROWS:(g + 1) * ROWS] = rotate(qraw[:, cols]).astype(jnp.bfloat16)

    def early(d, _):
        step(d)
        for e in range(2):
            rotate_q((d - 2) * 2 + e)
        return 0

    lax.fori_loop(2, half - 2, early, 0)

    q_row = kp[OWN][0:1]
    q_col = jnp.min(jnp.where(rows == lanes, jnp.broadcast_to(q_row, (ROWS, D)), FAR),
                    axis=1, keepdims=True)
    q_live = q_col < FAR

    def build_cap(first, last):
        for t in range(first // 2, last // 2):
            pair = jnp.where(lanes[0:1] < ROWS, kp[2 * t, 0:1], kp[2 * t + 1, 0:1])
            cap[:, t * D:(t + 1) * D] = jnp.where(
                jnp.broadcast_to(pair, (ROWS, D)) <= q_col, jnp.float32(jnp.inf), NEG)

    def scores(h, first, last):
        keys = kv[h, first:last, 0].reshape((last - first) * ROWS, D)
        s = lax.dot_general(rq[h], keys, (((1,), (1,)), ((), ())),
                            preferred_element_type=jnp.float32)
        c = cap[:, first * ROWS:last * ROWS]
        s = jnp.minimum(s, jnp.concatenate([c] * REP, axis=0))
        return s, jnp.max(s, axis=1, keepdims=True)

    def weigh(h, s, m, first, last):
        vals = kv[h, first:last, 1].reshape((last - first) * ROWS, D)
        w = jnp.exp2(s * SCALE - m * SCALE)
        return jnp.sum(w, axis=1, keepdims=True), jnp.dot(
            w.astype(jnp.bfloat16), vals, preferred_element_type=jnp.float32)

    def part_one(h):
        s, m = scores(h, 0, FIRST)
        total, o = weigh(h, s, m, 0, FIRST)
        o1[h] = o
        m1[h] = jnp.broadcast_to(m, (QROWS, D))
        l1[h] = jnp.broadcast_to(total, (QROWS, D))

    def part_two(h):
        s, m = scores(h, FIRST, n)
        m = jnp.maximum(m, m1[h][:, 0:1])
        total, o = weigh(h, s, m, FIRST, n)
        a = jnp.exp2((m1[h] - m) * SCALE)
        o = (o1[h] * a + o) / (l1[h] * a + total)
        parts = [jnp.where(q_live, o[g * ROWS:(g + 1) * ROWS], 0.0) for g in range(REP)]
        out_ref[:, pl.ds(pl.multiple_of(h * REP * D, D), REP * D)] = jnp.concatenate(
            parts, axis=1).astype(jnp.bfloat16)

    d = half - 2
    for r in BOTH:
        pcopy(d - 1, r).wait_recv()
        pcopy(d, r).start()
    build_cap(0, FIRST)

    def six(j, _):
        for e in range(2):
            h = 2 * j + e
            for r in BOTH:
                copy(h, d - 1, r).wait_recv()
                copy(h, d, r).start()
        part_one(j)
        return 0

    lax.fori_loop(0, KVH // 2, six, 0)
    for r in BOTH:
        pcopy(d, r).wait_recv()
    pcopy(d + 1, True).start()

    def seven(j, _):
        for e in range(2):
            h = 2 * j + e
            for r in BOTH:
                copy(h, d, r).wait_recv()
            copy(h, d + 1, e == 0).start()
        part_one(KVH // 2 + j)
        return 0

    lax.fori_loop(0, KVH // 2, seven, 0)
    pcopy(d + 1, True).wait_recv()
    build_cap(FIRST, n)

    def eight(j, _):
        for e in range(2):
            h = 2 * j + e
            copy(h, d + 1, e == 0).wait_recv()
            part_two(h)
        return 0

    lax.fori_loop(0, KVH // 2, eight, 0)

    for r in BOTH:
        pcopy(0, r).wait_send()
        for h in range(KVH):
            vcopy(h, r).wait_send()
            kcopy(h, r).wait_send()

    def drain(d, _):
        for r in BOTH:
            pcopy(d, r).wait_send()
            for h in range(KVH):
                copy(h, d, r).wait_send()
        return 0

    lax.fori_loop(1, half - 1, drain, 0)
    pcopy(half - 1, True).wait_send()
    for h in range(KVH):
        copy(h, half - 1, h % 2 == 0).wait_send()


def attend(n, *operands):
    vm = pl.BlockSpec(memory_space=pltpu.VMEM)
    hbm = pl.BlockSpec(memory_space=pl.ANY)
    dma = pltpu.SemaphoreType.DMA
    b16, f32, i32 = jnp.bfloat16, jnp.float32, jnp.int32
    half = n // 2
    return pl.pallas_call(
        functools.partial(kernel, n),
        out_shape=jax.ShapeDtypeStruct((ROWS, QH * D), b16),
        in_specs=[hbm, hbm, hbm, hbm, hbm, hbm],
        out_specs=vm,
        scratch_shapes=[
            pltpu.SMEM((1, 1, 1), i32),
            pltpu.VMEM((ROWS, KVH * D), b16),
            pltpu.VMEM((ROWS, KVH * D), b16),
            pltpu.VMEM((ROWS, QH * D), b16),
            pltpu.VMEM((1, ROWS), i32),
            pltpu.VMEM((1, D), f32),
            pltpu.VMEM((KVH, n, 2, ROWS, D), b16),
            pltpu.VMEM((n, 8, D), i32),
            pltpu.VMEM((KVH, QROWS, D), b16),
            pltpu.VMEM((ROWS, n * ROWS), f32),
            pltpu.VMEM((KVH, QROWS, D), f32),
            pltpu.VMEM((KVH, QROWS, D), f32),
            pltpu.VMEM((KVH, QROWS, D), f32),
            dma((6,)),
            dma((2, KVH, half)), dma((KVH, n)),
            dma((2, KVH)), dma((2, KVH)),
            dma((2, half)), dma((n,)),
        ],
        compiler_params=pltpu.CompilerParams(
            collective_id=0, has_side_effects=True, vmem_limit_bytes=56 * 1024 * 1024),
        name="gather_attend",
    )(*operands)


def on_device(queries, keys, values, positions, piece_lengths, dest_group, dest_offset):
    n = lax.axis_size("sp")
    groups = lax.axis_size("dp")
    mask = dest_group[0, 0] ^ lax.axis_index("dp")
    out = attend(n, piece_lengths, queries, keys, values,
                 positions.reshape(1, ROWS), jnp.asarray(frequencies()))
    out = lax.switch(mask, [
        functools.partial(lambda m, x: lax.ppermute(x, "dp", [(i, i ^ m) for i in range(groups)]), m)
        for m in range(groups)
    ], out)
    named = (mask >= 0) & (mask < groups)
    return jnp.where(named, out, jnp.zeros_like(out))


def solution(mesh):
    in_specs = (
        P(("dp", "sp"), None), P(("dp", "sp"), None), P(("dp", "sp"), None), P(("dp", "sp")),
        P("dp", "sp", None), P("dp", None), P("dp", "sp", None),
    )
    return jax.shard_map(on_device, mesh=mesh, in_specs=in_specs,
                         out_specs=P(("dp", "sp"), None), check_vma=False)
```
